1024 devices in a mesh: fsdp: 32 (over y, x_lo, core), ep: 32 (over x_hi, z).
Axes of the slice: x: 4 (x_hi: 2, x_lo: 2; x = x_hi * 2 + x_lo), y: 8, z: 16, core: 2. Of those that a mesh axis runs over, the one named last changes fastest.
Arguments:
- expert_ids: int32 [1024, 4], P('ep'), may hold values from 0 to 15, all different within a row; in each aligned block of 32 rows (0 to 31, 32 to 63, ...) at most 16 rows name the same one
- route_weights: float32 [1024, 4], P('ep'), may hold values from 0.1 to 1
- residual_grad: bfloat16 [1024, 6144], P('ep', 'fsdp'), may hold values from -6 to 6
- hidden_grad: bfloat16 [32, 512, 2688], P('ep'), may hold values from -6 to 6
- gate_pre: bfloat16 [32, 512, 2688], P('ep'), may hold values from -6 to 6
- up_pre: bfloat16 [32, 512, 2688], P('ep'), may hold values from -6 to 6
- gate_weight: bfloat16 [32, 6144, 2688], P('ep', 'fsdp'), may hold values from -0.0625 to 0.0625
- up_weight: bfloat16 [32, 6144, 2688], P('ep', 'fsdp'), may hold values from -0.0625 to 0.0625
- attn_context: bfloat16 [8192, 6144], P('fsdp', 'ep'), may hold values from -6 to 6
- attn_grad: bfloat16 [8192, 6144], P('fsdp'), may hold values from -6 to 6
Outputs:
- input_grad: bfloat16 [1024, 6144], P('ep', 'fsdp')
- proj_weight_grad: float32 [6144, 6144], P('ep', 'fsdp')
The draws below stay inside these ranges and needn't reach their ends.
Inputs may be any that keep to these rules, and one draw needn't show every extreme that they name: `expert_ids`: each row names 4 different experts. Among the rows of one ep index no expert is named more than 16 times, a bound that some block reaches.
All inputs are finite; a program needn't handle non-finite values.
Results may differ from the reference program's by a relative error of at most 0.005.
Values may be sent and summed in bfloat16 or wider, within the bound.
No kernel may reach another device: no remote copies, remote signals or barrier semaphores. Data moves between devices by JAX's collectives and lax.ppermute only.
A program may use at most 64 MiB of HBM per device.

```python
import math
import jax
import jax.numpy as jnp
import numpy as np
from jax import lax

D = 6144
FF = 10752
EXPERTS = 16
TOP = 4
CAP = 16
TOK_DEV = 32
HALF = 2688
SLOTS = 512
TOKENS = 1024
ATT_TOKENS = 8192
N_EP = 32


def with_spikes(result, own_key, source, target, blocks, factor):
    owner, partner = [(jnp.arange(result.shape[axis_at]) // (result.shape[axis_at] // blocks)).reshape([-1 if axis == axis_at else 1 for axis in range(result.ndim)]) for axis_at in (source, target)]
    chosen = jax.random.permutation(own_key, blocks)[partner]
    strong = (owner == chosen) | (owner == (partner + blocks // 2) % blocks)
    return jnp.where(strong, factor * result, result)


def steps_of(key, shape, split, smallest, top_value):
    level, own = 1.0, jax.random.fold_in(key, 6)
    for position, blocks in split:
        draws = jnp.exp(jax.random.uniform(jax.random.fold_in(own, position), (blocks,), jnp.float32, smallest / len(split), top_value / len(split)))
        level = level * jnp.repeat(draws, shape[position] // blocks).reshape([-1 if axis == position else 1 for axis in range(len(shape))])
    return level


def routed_block(stream_key, own, number, rows, count, top, reach, slope):
    order = jax.random.permutation(stream_key, count)
    crowded, usual = portions_of(count, rows * top, reach, slope, True), portions_of(count, rows * top, reach, slope, False)
    places = jnp.arange(count)

    def named(lengths, offset_by):
        used = int((lengths > 0).sum())
        fixed = max(1, used // 4)
        shifted = fixed + (places - fixed + offset_by * (used - fixed)) % max(1, count - fixed)
        return jnp.zeros((count,), jnp.int32).at[order[jnp.where(places < fixed, places, shifted)]].set(jnp.asarray(lengths, jnp.int32))

    lengths = jnp.where(number % 4 == 0, named(crowded, number // 4), named(usual, number - number // 4 - 1))
    mixed = jax.random.permutation(jax.random.fold_in(own, 3), count)
    donor, receiver = mixed[0:count // 2 * 2:2], mixed[1:count // 2 * 2:2]
    margin = jnp.minimum(lengths[donor] - 1, reach - lengths[receiver]) // 2
    margin = jnp.where((donor == order[0]) | (receiver == order[0]) | (lengths[receiver] == 0), 0, jnp.maximum(margin, 0))
    shifted = jax.random.randint(jax.random.fold_in(own, 4), (count // 2,), 0, 1 << 20) % (margin + 1)
    lengths = lengths.at[donor].add(-shifted).at[receiver].add(shifted)
    labels = jnp.searchsorted(jnp.cumsum(lengths), jnp.arange(rows * top), side="right").astype(jnp.int32)
    listing = labels.reshape(top, rows).T
    listing = listing[jax.random.permutation(jax.random.fold_in(own, 1), rows)]
    offset_by = jax.random.randint(jax.random.fold_in(own, 2), (rows, 1), 0, top)
    return jnp.take_along_axis(listing, (jnp.arange(top)[None, :] + offset_by) % top, axis=1)


def portions_of(amount, total, reach, skew, full):
    weights = [(1 << 20) // math.isqrt(grade ** skew) + 1 for grade in range(1, amount + 1)]
    largest = reach if full else min(reach, max(-(-total // amount), total * weights[0] // sum(weights)))
    least = 1 if total - largest >= amount - 1 else 0
    given, surplus = [largest] + [least] * (amount - 1), total - largest - least * (amount - 1)
    while surplus > 0:
        free = [i for i in range(1, amount) if given[i] < largest] or [i for i in range(1, amount) if given[i] < reach]
        whole, remaining = sum([weights[i] for i in free]), surplus
        for i in free:
            more = min(reach - given[i], max(1, remaining * weights[i] // whole), surplus)
            given[i] = given[i] + more
            surplus = surplus - more
    return np.array(given)


def scatter_about(stream_key, shape, width, bound, split=(), kind=jnp.bfloat16):
    result = jax.random.normal(stream_key, shape, jnp.float32) * width
    if len(split) > 0:
        result = steps_of(stream_key, shape, split, -0.22, 0.18) * result
    return jnp.clip(result, min=-bound, max=bound).astype(kind)


def noise_with(rng, extent, scale, most, split, heavy, kind=jnp.bfloat16):
    array = scale * jax.random.normal(rng, extent, jnp.float32)
    if split:
        array = array * steps_of(rng, extent, split, -0.22, 0.18)
    return jnp.clip(with_spikes(array, jax.random.fold_in(rng, 3), *heavy), -most, most).astype(kind)


def setup_inputs(seed: int = 0) -> dict:
    key_list = jax.random.split(jax.random.key(seed), 11)
    expert_ids_keys = jax.random.split(jax.random.fold_in(key_list[0], 1), TOKENS // TOK_DEV)
    expert_ids_turns = jax.random.permutation(jax.random.fold_in(key_list[0], 3), TOKENS // TOK_DEV)
    expert_ids = jax.vmap(lambda own, number: routed_block(jax.random.fold_in(key_list[0], 2), own, number, TOK_DEV, EXPERTS, TOP, CAP, 2))(expert_ids_keys, expert_ids_turns).reshape((TOKENS, TOP))
    route_weights = jnp.clip(jnp.exp(math.log(1.0) - 2.3025851 * jax.random.uniform(key_list[1], (TOKENS, TOP), jnp.float32) ** steps_of(key_list[1], (TOKENS, TOP), ((0, 32),), -0.2, 0.2)), 0.1, 1.0)
    residual_grad = scatter_about(key_list[2], (TOKENS, D), 1.0, 6.0, ((0, 32), (1, 32)))
    hidden_grad = scatter_about(key_list[3], (2 * EXPERTS, SLOTS, HALF), 1.0, 6.0, ((0, 32),))
    gate_pre = scatter_about(key_list[4], (2 * EXPERTS, SLOTS, HALF), 1.5, 6.0, ((0, 32),))
    up_pre = scatter_about(key_list[5], (2 * EXPERTS, SLOTS, HALF), 1.0, 6.0, ((0, 32),))
    gate_weight = scatter_about(key_list[6], (2 * EXPERTS, D, HALF), FF ** -0.5, 0.0625, ((0, 32), (1, 32)))
    up_weight = scatter_about(key_list[7], (2 * EXPERTS, D, HALF), FF ** -0.5, 0.0625, ((0, 32), (1, 32)))
    attn_context = scatter_about(key_list[8], (ATT_TOKENS, D), 1.0, 6.0, ((0, 32), (1, 32)))
    attn_grad = noise_with(key_list[9], (ATT_TOKENS, D), 1.0, 6.0, ((0, 32),), (0, 1, 32, 2.75))
    return dict(expert_ids=expert_ids, route_weights=route_weights, residual_grad=residual_grad, hidden_grad=hidden_grad, gate_pre=gate_pre, up_pre=up_pre, gate_weight=gate_weight, up_weight=up_weight, attn_context=attn_context, attn_grad=attn_grad)


def slot_table(expert_ids):
    flat = expert_ids.reshape(N_EP, TOK_DEV * TOP)
    onehot = (flat[:, :, None] == jnp.arange(EXPERTS, dtype=jnp.int32)[None, None, :]).astype(jnp.int32)
    before = jnp.cumsum(onehot, axis=1) - onehot
    return jnp.sum(before * onehot, axis=2).reshape(N_EP, TOK_DEV, TOP).astype(jnp.int32)


def reference(expert_ids, route_weights, residual_grad, hidden_grad, gate_pre, up_pre, gate_weight, up_weight, attn_context, attn_grad):
    gate = gate_pre.astype(jnp.float32)
    upper = up_pre.astype(jnp.float32)
    grads = hidden_grad.astype(jnp.float32)
    sig = jax.nn.sigmoid(gate)
    up_term = (grads * gate * sig).astype(jnp.bfloat16)
    gate_term = (grads * upper * sig * (1.0 + gate * (1.0 - sig))).astype(jnp.bfloat16)

    def one_block(items):
        gterm, uterm, gweight, uweight = items
        first = jnp.dot(gterm, gweight.T, preferred_element_type=jnp.float32)
        second = jnp.dot(uterm, uweight.T, preferred_element_type=jnp.float32)
        return (first + second).astype(jnp.bfloat16)

    expert_rows = lax.map(one_block, (gate_term, up_term, gate_weight, up_weight))
    table = expert_rows.astype(jnp.float32).reshape(2 * EXPERTS, N_EP, CAP, D)
    slots = slot_table(expert_ids)
    ids = expert_ids.reshape(N_EP, TOK_DEV, TOP)
    source = jnp.arange(N_EP, dtype=jnp.int32)[:, None, None]
    low_half = table[2 * ids, source, slots]
    high_half = table[2 * ids + 1, source, slots]
    weights = route_weights.reshape(N_EP, TOK_DEV, TOP, 1)
    combined = jnp.sum(weights * (low_half + high_half), axis=2).reshape(TOKENS, D)
    input_grad = (residual_grad.astype(jnp.float32) + combined).astype(jnp.bfloat16)
    proj_weight_grad = jnp.dot(attn_context.T, attn_grad, preferred_element_type=jnp.float32)
    return input_grad, proj_weight_grad
```

```python
import functools

import jax
import jax.numpy as jnp
from jax import lax
from jax.experimental import pallas as pl
from jax.experimental.pallas import tpu as pltpu
from jax.sharding import PartitionSpec as P

F32, BF16 = jnp.float32, jnp.bfloat16
LANES = 128
MIB = 1 << 20


def params(limit=32 * MIB):
    return pltpu.CompilerParams(vmem_limit_bytes=limit)


def whole():
    return pl.BlockSpec(memory_space=pltpu.VMEM)


def low_lanes(rows):
    return lax.broadcasted_iota(jnp.int32, (rows, LANES), 1) < LANES // 2


def proj_partial_kernel(core_ref, ctx_ref, grad_ref, own_ref, send_ref):
    rows = ctx_ref.shape[1]
    half = rows // 2
    full = rows + half
    core = core_ref[0]
    left = low_lanes(half)
    for pair in range(grad_ref.shape[1] // (2 * rows)):
        cols = grad_ref[:, pair * 2 * rows:(pair + 1) * 2 * rows]
        prod = lax.dot_general(
            ctx_ref[...], cols, (((0,), (0,)), ((), ())), preferred_element_type=F32
        )
        middle = prod[:, LANES:2 * LANES]
        upper, lower = middle[:half], middle[half:]
        even = jnp.concatenate(
            [prod[:, :LANES], jnp.where(left, upper, pltpu.roll(lower, LANES // 2, 1))], axis=0
        )
        odd = jnp.concatenate(
            [prod[:, 2 * LANES:], jnp.where(left, pltpu.roll(upper, LANES // 2, 1), lower)], axis=0
        )
        at = slice(pair * full, (pair + 1) * full)
        own_ref[at, :] = jnp.where(core == 0, even, odd).astype(own_ref.dtype)
        send_ref[at, :] = jnp.where(core == 0, odd, even).astype(send_ref.dtype)


def proj_partial(core, ctx, grad):
    tokens, rows = ctx.shape
    steps = 4
    width = grad.shape[1] // steps
    out_rows = grad.shape[1] * rows // LANES
    return pl.pallas_call(
        proj_partial_kernel,
        grid=(steps,),
        in_specs=[
            pl.BlockSpec(memory_space=pltpu.SMEM),
            pl.BlockSpec((tokens, rows), lambda s: (0, 0)),
            pl.BlockSpec((tokens, width), lambda s: (0, s)),
        ],
        out_specs=[pl.BlockSpec((out_rows // 2 // steps, LANES), lambda s: (s, 0))] * 2,
        out_shape=[jax.ShapeDtypeStruct((out_rows // 2, LANES), BF16)] * 2,
        compiler_params=params(),
        cost_estimate=pl.CostEstimate(
            flops=2 * tokens * rows * grad.shape[1], bytes_accessed=6 * MIB, transcendentals=0
        ),
        name="proj_partial",
    )(core, ctx, grad)


def chip_sum_kernel(side_ref, own_ref, got_ref, keep_ref, send_ref, by_y_ref, *, rows):
    side = side_ref[0]
    half = rows // 2
    full = rows + half
    for y in range(keep_ref.shape[0] // rows):
        mine = pl.ds(pl.multiple_of((2 * y + side) * full, 16), rows)
        other = pl.ds(pl.multiple_of((2 * y + 1 - side) * full, 16), rows)
        at = slice(y * rows, (y + 1) * rows)
        keep_ref[at, :] = own_ref[mine, :] + got_ref[mine, :].astype(F32)
        send_ref[at, :] = (own_ref[other, :] + got_ref[other, :].astype(F32)).astype(BF16)
        for x in range(2):
            start = (2 * y + x) * full + rows
            block = slice(start, start + half)
            to = slice((2 * y + x) * half, (2 * y + x + 1) * half)
            by_y_ref[to, :] = (own_ref[block, :] + got_ref[block, :].astype(F32)).astype(BF16)


def add_kernel(own_ref, got_ref, out_ref):
    out_ref[...] = (own_ref[...] + got_ref[...].astype(F32)).astype(out_ref.dtype)


def y_sum_kernel(side_ref, got_ref, keep_ref, send_ref, *, parts):
    rows = got_ref.shape[0] // parts
    half = rows // 2
    side = side_ref[0]

    def total(start):
        acc = got_ref[pl.ds(start, half), :].astype(F32)
        for part in range(1, parts):
            acc += got_ref[pl.ds(part * rows + start, half), :].astype(F32)
        return acc

    keep_ref[...] = total(pl.multiple_of(side * half, 16))
    send_ref[...] = total(pl.multiple_of((1 - side) * half, 16)).astype(BF16)


def proj_final_kernel(core_ref, main_ref, keep_ref, got_ref, out_ref, *, parts):
    rows = main_ref.shape[0] // parts
    core = core_ref[0]
    acc = main_ref[:rows, :].astype(F32)
    for part in range(1, parts):
        acc += main_ref[part * rows:(part + 1) * rows, :].astype(F32)
    packed = keep_ref[...] + got_ref[...].astype(F32)
    half = jnp.concatenate([packed, pltpu.roll(packed, LANES // 2, 1)], axis=0)
    turned = pltpu.roll(acc, LANES // 2, 1)
    out_ref[:, :LANES] = jnp.where(core == 0, acc, jnp.where(low_lanes(rows), half, turned))
    out_ref[:, LANES:] = jnp.where(core == 0, half, turned)[:, :rows - LANES]


def expert_kernel(hid_ref, gate_ref, up_ref, gw_ref, uw_ref, out_ref, acc_ref):
    step = pl.program_id(0)
    hid = hid_ref[...].astype(F32)
    gate = gate_ref[...].astype(F32)
    sig = 0.5 * jnp.tanh(0.5 * gate) + 0.5
    scaled = hid * sig
    up_term = (scaled * gate).astype(BF16)
    gate_term = (scaled * up_ref[...].astype(F32) * (1.0 + gate * (1.0 - sig))).astype(BF16)
    dims = (((1,), (1,)), ((), ()))
    prod = lax.dot_general(gate_term, gw_ref[...], dims, preferred_element_type=F32)
    prod += lax.dot_general(up_term, uw_ref[...], dims, preferred_element_type=F32)

    @pl.when(step == 0)
    def _():
        acc_ref[...] = prod

    @pl.when(step > 0)
    def _():
        acc_ref[...] += prod

    @pl.when(step == pl.num_programs(0) - 1)
    def _():
        slots, width = acc_ref.shape
        rest = width - LANES
        groups = slots // 16
        main = acc_ref[:, :LANES].reshape(groups, 16, LANES)
        side = acc_ref[:, LANES:].reshape(groups, 2, 8, rest)
        side = jnp.concatenate([side[:, 0], side[:, 1]], axis=-1)
        packed = jnp.concatenate([main, side], axis=1)
        out_ref[...] = packed.reshape(groups * 24, LANES).astype(BF16)


def expert_rows(hid, gate, up, gw, uw):
    slots, hidden = hid.shape
    width = gw.shape[0]
    block = 384
    steps = hidden // block
    rows_spec = pl.BlockSpec((slots, block), lambda s: (0, s))
    weight_spec = pl.BlockSpec((width, block), lambda s: (0, s))
    out_rows = slots * width // LANES
    return pl.pallas_call(
        expert_kernel,
        grid=(steps,),
        in_specs=[rows_spec] * 3 + [weight_spec] * 2,
        out_specs=pl.BlockSpec((out_rows, LANES), lambda s: (0, 0)),
        out_shape=jax.ShapeDtypeStruct((out_rows, LANES), BF16),
        scratch_shapes=[pltpu.VMEM((slots, width), F32)],
        compiler_params=params(),
        cost_estimate=pl.CostEstimate(
            flops=4 * slots * hidden * width,
            bytes_accessed=2 * hidden * (3 * slots + 2 * width),
            transcendentals=slots * hidden,
        ),
        name="expert_rows",
    )(hid, gate, up, gw, uw)


def combine_kernel(ids_ref, weights_ref, residual_ref, got_ref, out_ref):
    tokens, top = ids_ref.shape
    blocks = got_ref.shape[0] // 24
    experts = blocks // 2
    ids, weights = ids_ref[...], weights_ref[...]
    row = lax.broadcasted_iota(jnp.int32, (tokens, tokens), 0)
    col = lax.broadcasted_iota(jnp.int32, (tokens, tokens), 1)
    earlier = (col < row).astype(F32)

    def picks(per_expert):
        lane = lax.broadcasted_iota(jnp.int32, (tokens, experts * per_expert), 1)
        named = jnp.zeros(lane.shape, F32)
        weight = jnp.zeros(lane.shape, F32)
        for k in range(top):
            hit = ids[:, k:k + 1] == lane // per_expert
            named += hit.astype(F32)
            weight += jnp.where(hit, weights[:, k:k + 1], 0.0)
        before = jnp.dot(earlier, named, preferred_element_type=F32)
        slot = (lane % per_expert).astype(F32)
        return [
            jnp.where(before == slot + base, weight, 0.0) for base in range(0, 16, per_expert)
        ]

    got = got_ref[...].astype(F32).reshape(experts, 2, 24, LANES)
    both = got[:, 0] + got[:, 1]
    main = both[:, :16].reshape(experts * 16, LANES)
    side = both[:, 16:].reshape(experts * 8, LANES)
    dot = functools.partial(
        jnp.dot, precision=lax.Precision.HIGHEST, preferred_element_type=F32
    )
    first, second = picks(8)
    main_sum = dot(picks(16)[0], main)
    side_sum = dot(first, side) + pltpu.roll(dot(second, side), LANES // 2, 1)
    rest = out_ref.shape[1] - LANES
    out_ref[:, :LANES] = (residual_ref[:, :LANES].astype(F32) + main_sum).astype(BF16)
    out_ref[:, LANES:] = (residual_ref[:, LANES:].astype(F32) + side_sum[:, :rest]).astype(BF16)


def shards(ids, weights, residual, hid, gate, up, gw, uw, ctx, grad, n_fsdp):
    me = lax.axis_index("fsdp")
    core = (me & 1).reshape(1)
    side = ((me >> 1) & 1).reshape(1)
    rows = ctx.shape[1]
    half = rows // 2
    n_y = n_fsdp // 4
    y_groups = [[4 * y + c for y in range(n_y)] for c in range(4)]
    along_core = [(j, j ^ 1) for j in range(n_fsdp)]
    along_x = [(j, j ^ 2) for j in range(n_fsdp)]

    def swap(array, pairs):
        return lax.ppermute(array, "fsdp", pairs)

    def to_y(array):
        return lax.all_to_all(
            array, "fsdp", 0, 0, axis_index_groups=y_groups, tiled=True
        )

    own, send = proj_partial(core, ctx, grad)
    got = swap(send, along_core)
    rows_out = expert_rows(hid[0], gate[0], up[0], gw[0], uw[0])
    received = lax.all_to_all(rows_out, "ep", 0, 0, tiled=True)

    smem = pl.BlockSpec(memory_space=pltpu.SMEM)
    wide = jax.ShapeDtypeStruct((n_y * rows, LANES), BF16)
    keep, x_send, by_y = pl.pallas_call(
        functools.partial(chip_sum_kernel, rows=rows),
        in_specs=[smem, whole(), whole()],
        out_specs=[whole()] * 3,
        out_shape=[jax.ShapeDtypeStruct(wide.shape, F32), wide, wide],
        compiler_params=params(),
        name="chip_sum",
    )(side, own, got)
    x_got = swap(x_send, along_x)
    side_parts = to_y(by_y)
    main_send = pl.pallas_call(
        add_kernel,
        in_specs=[whole()] * 2,
        out_specs=whole(),
        out_shape=wide,
        compiler_params=params(),
        name="x_sum",
    )(keep, x_got)
    main_parts = to_y(main_send)
    side_keep, side_send = pl.pallas_call(
        functools.partial(y_sum_kernel, parts=n_y),
        in_specs=[smem, whole()],
        out_specs=[whole()] * 2,
        out_shape=[
            jax.ShapeDtypeStruct((half, LANES), F32),
            jax.ShapeDtypeStruct((half, LANES), BF16),
        ],
        compiler_params=params(),
        name="y_sum",
    )(side, side_parts)
    side_got = swap(side_send, along_x)

    input_grad = pl.pallas_call(
        combine_kernel,
        in_specs=[whole()] * 4,
        out_specs=whole(),
        out_shape=jax.ShapeDtypeStruct(residual.shape, BF16),
        compiler_params=params(),
        name="combine",
    )(ids, weights, residual, received)
    proj_weight_grad = pl.pallas_call(
        functools.partial(proj_final_kernel, parts=n_y),
        in_specs=[smem] + [whole()] * 3,
        out_specs=whole(),
        out_shape=jax.ShapeDtypeStruct((rows, rows), F32),
        compiler_params=params(),
        name="proj_final",
    )(core, main_parts, side_keep, side_got)
    return input_grad, proj_weight_grad


def solution(mesh):
    return jax.shard_map(
        functools.partial(shards, n_fsdp=mesh.shape["fsdp"]),
        mesh=mesh,
        in_specs=(
            P("ep", None),
            P("ep", None),
            P("ep", "fsdp"),
            P("ep", None, None),
            P("ep", None, None),
            P("ep", None, None),
            P("ep", "fsdp", None),
            P("ep", "fsdp", None),
            P("fsdp", "ep"),
            P("fsdp", None),
        ),
        out_specs=(P("ep", "fsdp"), P("ep", "fsdp")),
        check_vma=False,
    )
```

```python
import functools

import jax
import jax.numpy as jnp
from jax import lax
from jax.experimental import pallas as pl
from jax.experimental.pallas import tpu as pltpu
from jax.sharding import PartitionSpec as P

F32, BF16 = jnp.float32, jnp.bfloat16
LANES = 128
MIB = 1 << 20
EXPERTS = 16
GRAD_PARTS = 2
HIDDEN_PART = 768


def params(limit):
    return pltpu.CompilerParams(vmem_limit_bytes=limit)


def whole():
    return pl.BlockSpec(memory_space=pltpu.VMEM)


def in_hbm():
    return pl.BlockSpec(memory_space=pltpu.HBM)


def hold(array):
    return pltpu.with_memory_space_constraint(array, pltpu.HBM)


def low_lanes(rows):
    return lax.broadcasted_iota(jnp.int32, (rows, LANES), 1) < LANES // 2


def write_picks(ids, weights, picks_ref):
    top, tokens = ids.shape
    row = lax.broadcasted_iota(jnp.int32, (tokens, tokens), 0)
    col = lax.broadcasted_iota(jnp.int32, (tokens, tokens), 1)
    earlier = (row < col).astype(F32)
    at = 0
    for per_expert in (16, 8):
        line = lax.broadcasted_iota(jnp.int32, (EXPERTS * per_expert, tokens), 0)
        expert = line // per_expert
        named = jnp.zeros(line.shape, F32)
        weight = jnp.zeros(line.shape, F32)
        for k in range(top):
            hit = ids[k:k + 1, :] == expert
            named += hit.astype(F32)
            weight += jnp.where(hit, weights[k:k + 1, :], 0.0)
        before = jnp.dot(named, earlier, preferred_element_type=F32)
        for base in range(0, 16, per_expert):
            slot = (line % per_expert + base).astype(F32)
            picks_ref[at:at + line.shape[0], :] = jnp.where(before == slot, weight, 0.0)
            at += line.shape[0]


def front_kernel(core_ref, ids_hbm, weights_hbm, residual_hbm, ctx_hbm, grad_hbm,
                 hid_hbm, gate_hbm, up_hbm, gw_hbm, uw_hbm,
                 own_ref, send_ref, rows_ref, picks_ref, residual_ref,
                 ids, weights, ctx, grad, hid, gate, up, gw, uw, gate_term, up_term, acc, sems):
    rows = ctx.shape[0]
    half = rows // 2
    full = rows + half
    slots, hidden = hid.shape
    cuts = range(0, hidden, HIDDEN_PART)
    copies = []

    def begin(source, target):
        copy = pltpu.make_async_copy(source, target, sems.at[len(copies)])
        copies.append(copy)
        copy.start()
        return copy

    def fetch(source, target, start, size):
        at = pl.ds(start, size)
        return begin(source.at[:, at], target.at[:, at])

    routes = [begin(ids_hbm, ids), begin(weights_hbm, weights)]
    width = grad.shape[1] // GRAD_PARTS
    ctx_copy = begin(ctx_hbm, ctx)
    grad_copies = [fetch(grad_hbm, grad, part * width, width) for part in range(GRAD_PARTS)]
    pairs = ((hid_hbm, hid), (gate_hbm, gate), (up_hbm, up), (gw_hbm, gw), (uw_hbm, uw))
    expert_copies = [
        [fetch(source, target, cut, min(HIDDEN_PART, hidden - cut)) for source, target in pairs]
        for cut in cuts
    ]
    residual_copy = begin(residual_hbm, residual_ref)

    for copy in routes:
        copy.wait()
    write_picks(ids[...], weights[...], picks_ref)
    ctx_copy.wait()
    core = core_ref[0]
    left = low_lanes(half)
    each = width // (2 * rows)
    for part in range(GRAD_PARTS):
        grad_copies[part].wait()
        for pair in range(part * each, (part + 1) * each):
            prod = jnp.dot(
                ctx[...], grad[:, pair * 2 * rows:(pair + 1) * 2 * rows],
                preferred_element_type=F32,
            )
            even, middle, odd = (prod[:, k * LANES:(k + 1) * LANES] for k in range(3))
            upper, lower = middle[:half], middle[half:]
            even_side = jnp.where(left, upper, pltpu.roll(lower, LANES // 2, 1))
            odd_side = jnp.where(left, pltpu.roll(upper, LANES // 2, 1), lower)
            main = slice(pair * full, pair * full + rows)
            rest = slice(pair * full + rows, (pair + 1) * full)
            own_ref[main, :] = jnp.where(core == 0, even, odd).astype(BF16)
            own_ref[rest, :] = jnp.where(core == 0, even_side, odd_side).astype(BF16)
            send_ref[main, :] = jnp.where(core == 0, odd, even).astype(BF16)
            send_ref[rest, :] = jnp.where(core == 0, odd_side, even_side).astype(BF16)

    dims = (((1,), (1,)), ((), ()))
    for copies_of_part, cut in zip(expert_copies, cuts):
        for copy in copies_of_part:
            copy.wait()
        cols = slice(cut, min(cut + HIDDEN_PART, hidden))
        for start in range(0, slots, 64):
            at = slice(start, start + 64)
            h = hid[at, cols].astype(F32)
            g = gate[at, cols].astype(F32)
            sig = 0.5 * jnp.tanh(0.5 * g) + 0.5
            silu = g * sig
            up_term[at, cols] = (h * silu).astype(BF16)
            gate_term[at, cols] = (
                h * up[at, cols].astype(F32) * (sig * (1.0 + g - silu))
            ).astype(BF16)
        prod = lax.dot_general(
            gate_term[:, cols], gw[:, cols], dims, preferred_element_type=F32
        ) + lax.dot_general(up_term[:, cols], uw[:, cols], dims, preferred_element_type=F32)
        acc[...] = prod if cut == 0 else acc[...] + prod
    rest = acc.shape[1] - LANES
    groups = slots // 16
    main = acc[:, :LANES].reshape(groups, 16, LANES)
    side = acc[:, LANES:].reshape(groups, 2, 8, rest)
    side = jnp.concatenate([side[:, 0], side[:, 1]], axis=-1)
    packed = jnp.concatenate([main, side], axis=1)
    rows_ref[...] = packed.reshape(groups * 24, LANES).astype(BF16)
    residual_copy.wait()


def front(core, ids, weights, residual, ctx, grad, *experts):
    rows, tokens = ctx.shape
    top, routed = ids.shape
    out_rows = grad.shape[1] * rows // LANES // 2
    slots, hidden = experts[0].shape
    arrays = (ctx, grad, *experts)
    pick_rows = 2 * 16 * EXPERTS
    return pl.pallas_call(
        front_kernel,
        in_specs=[pl.BlockSpec(memory_space=pltpu.SMEM)] + [in_hbm()] * 10,
        out_specs=[whole()] * 5,
        out_shape=[jax.ShapeDtypeStruct((out_rows, LANES), BF16)] * 2
        + [
            jax.ShapeDtypeStruct((slots * rows // LANES, LANES), BF16),
            jax.ShapeDtypeStruct((pick_rows, routed), F32),
            jax.ShapeDtypeStruct(residual.shape, BF16),
        ],
        scratch_shapes=[pltpu.VMEM((top, routed), jnp.int32), pltpu.VMEM((top, routed), F32)]
        + [pltpu.VMEM(array.shape, BF16) for array in arrays]
        + [pltpu.VMEM((slots, hidden), BF16)] * 2
        + [
            pltpu.VMEM((slots, rows), F32),
            pltpu.SemaphoreType.DMA((4 + GRAD_PARTS + 5 * pl.cdiv(hidden, HIDDEN_PART),)),
        ],
        compiler_params=params(40 * MIB),
        cost_estimate=pl.CostEstimate(
            flops=2 * tokens * rows * grad.shape[1] + 4 * slots * hidden * rows,
            bytes_accessed=14 * MIB,
            transcendentals=slots * hidden,
        ),
        name="front",
    )(core, *map(hold, (ids, weights, residual, *arrays)))


def chip_sum_kernel(place_ref, own_ref, got_ref, _, keep_ref, *send_refs, full):
    send_refs = send_refs[:3]
    place = place_ref[0]
    for y in range(keep_ref.shape[0] // full):
        at = slice(y * full, (y + 1) * full)
        for turn, ref in enumerate((keep_ref, *send_refs)):
            start = pl.multiple_of((4 * y + (place ^ turn)) * full, 32)
            block = pl.ds(start, full)
            total = own_ref[block, :].astype(F32) + got_ref[block, :].astype(F32)
            ref[at, :] = total.astype(ref.dtype)


def square_sum_kernel(y_ref, keep_ref, *refs, full):
    got, out = refs[:3], refs[3:]
    parts = keep_ref.shape[0] // full
    for step in range(parts):
        start = pl.multiple_of(((y_ref[0] + step) & (parts - 1)) * full, 32)
        block = pl.ds(start, full)
        total = keep_ref[block, :]
        for ref in got:
            total += ref[block, :].astype(F32)
        out[step][...] = total.astype(out[step].dtype)


def proj_final_kernel(core_ref, keep_ref, *refs):
    got, out_ref = refs[:-1], refs[-1]
    rows = out_ref.shape[0]
    core = core_ref[0]
    total = keep_ref[...]
    for ref in got:
        total += ref[...].astype(F32)
    main, packed = total[:rows], total[rows:]
    half = jnp.concatenate([packed, pltpu.roll(packed, LANES // 2, 1)], axis=0)
    turned = pltpu.roll(main, LANES // 2, 1)
    out_ref[:, :LANES] = jnp.where(core == 0, main, jnp.where(low_lanes(rows), half, turned))
    out_ref[:, LANES:] = jnp.where(core == 0, half, turned)[:, :rows - LANES]


def combine_kernel(picks_ref, residual_ref, got_ref, out_ref):
    experts = got_ref.shape[0] // 48
    got = got_ref[...].astype(F32).reshape(experts, 2, 24, LANES)
    both = got[:, 0] + got[:, 1]
    main = both[:, :16].reshape(experts * 16, LANES)
    side = both[:, 16:].reshape(experts * 8, LANES)

    def dot(start, values):
        return lax.dot_general(
            picks_ref[start:start + values.shape[0], :], values, (((0,), (0,)), ((), ())),
            precision=lax.Precision.HIGHEST, preferred_element_type=F32,
        )

    main_sum = dot(0, main)
    upper = dot(experts * 16, side)
    lower = dot(experts * 24, side)
    side_sum = upper + pltpu.roll(lower, LANES // 2, 1)
    rest = out_ref.shape[1] - LANES
    out_ref[:, :LANES] = (residual_ref[:, :LANES].astype(F32) + main_sum).astype(BF16)
    out_ref[:, LANES:] = (residual_ref[:, LANES:].astype(F32) + side_sum[:, :rest]).astype(BF16)


def shards(ids, weights, residual, hid, gate, up, gw, uw, ctx, grad, n_fsdp):
    me = lax.axis_index("fsdp")
    core = (me & 1).reshape(1)
    place = ((me >> 1) & 3).reshape(1)
    y2 = (me >> 3).reshape(1)
    rows = ctx.shape[1]
    full = rows * rows // LANES
    parts = n_fsdp // 8
    smem = pl.BlockSpec(memory_space=pltpu.SMEM)

    def swap(array, bits):
        return lax.ppermute(array, "fsdp", [(j, j ^ bits) for j in range(n_fsdp)])

    def shift(array, step):
        return lax.ppermute(
            array, "fsdp", [(j, (j + 8 * step) % n_fsdp) for j in range(n_fsdp)]
        )

    experts = (hid[0], gate[0], up[0], gw[0], uw[0])
    own, send, rows_out, picks, residual = front(
        core, ids.T, weights.T, residual, ctx.T, grad, *experts
    )
    got = swap(send, 1)

    quarter = jax.ShapeDtypeStruct((parts * full, LANES), BF16)
    keep, *square_send, rows_out = pl.pallas_call(
        functools.partial(chip_sum_kernel, full=full),
        in_specs=[smem, whole(), whole(), pl.BlockSpec(memory_space=pl.ANY)],
        out_specs=[whole()] * 4 + [pl.BlockSpec(memory_space=pl.ANY)],
        out_shape=[jax.ShapeDtypeStruct(quarter.shape, F32)] + [quarter] * 3
        + [jax.ShapeDtypeStruct(rows_out.shape, BF16)],
        input_output_aliases={3: 4},
        compiler_params=params(4 * MIB),
        name="chip_sum",
    )(place, own, got, rows_out)
    square_got = [swap(square_send[k - 1], 2 * k) for k in (1, 3, 2)]
    received = lax.all_to_all(
        rows_out.reshape(-1, 24, LANES), "ep", 0, 0, tiled=True
    ).reshape(rows_out.shape)
    block = jax.ShapeDtypeStruct((full, LANES), BF16)
    keep, *y_send = pl.pallas_call(
        functools.partial(square_sum_kernel, full=full),
        in_specs=[smem] + [whole()] * 4,
        out_specs=[whole()] * parts,
        out_shape=[jax.ShapeDtypeStruct(block.shape, F32)] + [block] * (parts - 1),
        compiler_params=params(4 * MIB),
        cost_estimate=pl.CostEstimate(flops=10**10, bytes_accessed=MIB, transcendentals=0),
        name="square_sum",
    )(y2, keep, *square_got)
    y_got = [shift(y_send[k - 1], k) for k in (2, 1, 3)]

    input_grad = pl.pallas_call(
        combine_kernel,
        in_specs=[whole()] * 3,
        out_specs=whole(),
        out_shape=jax.ShapeDtypeStruct(residual.shape, BF16),
        compiler_params=params(8 * MIB),
        name="combine",
    )(picks, residual, received)
    proj_weight_grad = pl.pallas_call(
        proj_final_kernel,
        in_specs=[smem] + [whole()] * parts,
        out_specs=whole(),
        out_shape=jax.ShapeDtypeStruct((rows, rows), F32),
        compiler_params=params(4 * MIB),
        name="proj_final",
    )(core, keep, *y_got)
    return input_grad, proj_weight_grad


def solution(mesh):
    return jax.shard_map(
        functools.partial(shards, n_fsdp=mesh.shape["fsdp"]),
        mesh=mesh,
        in_specs=(
            P("ep", None),
            P("ep", None),
            P("ep", "fsdp"),
            P("ep", None, None),
            P("ep", None, None),
            P("ep", None, None),
            P("ep", "fsdp", None),
            P("ep", "fsdp", None),
            P("fsdp", "ep"),
            P("fsdp", None),
        ),
        out_specs=(P("ep", "fsdp"), P("ep", "fsdp")),
        check_vma=False,
    )
```

```python
import functools

import jax
import jax.numpy as jnp
from jax import lax
from jax.experimental import pallas as pl
from jax.experimental.pallas import tpu as pltpu
from jax.sharding import PartitionSpec as P

F32, BF16 = jnp.float32, jnp.bfloat16
LANES = 128
MIB = 1 << 20
EXPERTS = 16
GRAD_PARTS = 2
HIDDEN_CUTS = (0, 384, 1152, 1920)


def params(limit):
    return pltpu.CompilerParams(vmem_limit_bytes=limit)


def whole():
    return pl.BlockSpec(memory_space=pltpu.VMEM)


def in_hbm():
    return pl.BlockSpec(memory_space=pltpu.HBM)


def hold(array):
    return pltpu.with_memory_space_constraint(array, pltpu.HBM)


def low_lanes(rows):
    return lax.broadcasted_iota(jnp.int32, (rows, LANES), 1) < LANES // 2


def write_picks(ids, weights, picks_ref):
    top, tokens = ids.shape
    row = lax.broadcasted_iota(jnp.int32, (tokens, tokens), 0)
    col = lax.broadcasted_iota(jnp.int32, (tokens, tokens), 1)
    earlier = (row < col).astype(F32)
    at = 0
    for per_expert in (16, 8):
        line = lax.broadcasted_iota(jnp.int32, (EXPERTS * per_expert, tokens), 0)
        expert = line // per_expert
        named = jnp.zeros(line.shape, F32)
        weight = jnp.zeros(line.shape, F32)
        for k in range(top):
            hit = ids[k:k + 1, :] == expert
            named += hit.astype(F32)
            weight += jnp.where(hit, weights[k:k + 1, :], 0.0)
        before = jnp.dot(named, earlier, preferred_element_type=F32)
        for base in range(0, 16, per_expert):
            slot = (line % per_expert + base).astype(F32)
            picks_ref[at:at + line.shape[0], :] = jnp.where(before == slot, weight, 0.0)
            at += line.shape[0]


def front_kernel(core_ref, ids_hbm, weights_hbm, ctx_hbm, grad_hbm, *refs):
    residual_hbm, own_ref, send_ref, picks_ref, residual_ref = refs[:5]
    ids, weights, ctx, grad, packed, sems = refs[5:]
    rows = ctx.shape[0]
    half = rows // 2
    full = rows + half
    width = grad.shape[1] // GRAD_PARTS
    copies = []

    def begin(source, target):
        copy = pltpu.make_async_copy(source, target, sems.at[len(copies)])
        copies.append(copy)
        copy.start()
        return copy

    small = [begin(ids_hbm, ids), begin(weights_hbm, weights), begin(ctx_hbm, ctx)]
    parts = [pl.ds(part * width, width) for part in range(GRAD_PARTS)]
    parts = [begin(grad_hbm.at[:, cols], grad.at[:, cols]) for cols in parts]
    residual = begin(residual_hbm, residual_ref)

    for copy in small:
        copy.wait()
    write_picks(ids[...], weights[...], picks_ref)
    core = core_ref[0]
    left = low_lanes(half)
    each = width // (2 * rows)
    leaving = []
    for part in range(GRAD_PARTS):
        parts[part].wait()
        for pair in range(part * each, (part + 1) * each):
            prod = jnp.dot(
                ctx[...], grad[:, pair * 2 * rows:(pair + 1) * 2 * rows],
                preferred_element_type=F32,
            )
            even, middle, odd = (prod[:, k * LANES:(k + 1) * LANES] for k in range(3))
            upper, lower = middle[:half], middle[half:]
            even_side = jnp.where(left, upper, pltpu.roll(lower, LANES // 2, 1))
            odd_side = jnp.where(left, pltpu.roll(upper, LANES // 2, 1), lower)
            main = slice(pair * full, pair * full + rows)
            rest = slice(pair * full + rows, (pair + 1) * full)
            own_ref[main, :] = jnp.where(core == 0, even, odd).astype(BF16)
            own_ref[rest, :] = jnp.where(core == 0, even_side, odd_side).astype(BF16)
            packed[main, :] = jnp.where(core == 0, odd, even).astype(BF16)
            packed[rest, :] = jnp.where(core == 0, odd_side, even_side).astype(BF16)
        done = pl.ds(part * each * full, each * full)
        leaving.append(begin(packed.at[done, :], send_ref.at[done, :]))
    for copy in leaving:
        copy.wait()
    residual.wait()


def front(core, ids, weights, ctx, grad, residual):
    rows, tokens = ctx.shape
    top, routed = ids.shape
    out_rows = grad.shape[1] * rows // LANES // 2
    return pl.pallas_call(
        front_kernel,
        in_specs=[pl.BlockSpec(memory_space=pltpu.SMEM)] + [in_hbm()] * 5,
        out_specs=[whole(), in_hbm(), whole(), whole()],
        out_shape=[jax.ShapeDtypeStruct((out_rows, LANES), BF16)] * 2
        + [
            jax.ShapeDtypeStruct((2 * 16 * EXPERTS, routed), F32),
            jax.ShapeDtypeStruct(residual.shape, BF16),
        ],
        scratch_shapes=[
            pltpu.VMEM((top, routed), jnp.int32),
            pltpu.VMEM((top, routed), F32),
            pltpu.VMEM(ctx.shape, BF16),
            pltpu.VMEM(grad.shape, BF16),
            pltpu.VMEM((out_rows, LANES), BF16),
            pltpu.SemaphoreType.DMA((4 + 2 * GRAD_PARTS,)),
        ],
        compiler_params=params(10 * MIB),
        cost_estimate=pl.CostEstimate(
            flops=2 * tokens * rows * grad.shape[1], bytes_accessed=6 * MIB, transcendentals=0
        ),
        name="front",
    )(core, *map(hold, (ids, weights, ctx, grad, residual)))


def expert_kernel(core_ref, *refs):
    far, out_ref, near, (gate_term, up_term, acc, sems) = refs[:5], refs[5], refs[6:11], refs[11:]
    hid_ref, gate_ref, up_ref, gw_ref, uw_ref = near
    slots, hidden = hid_ref.shape
    cuts = [*HIDDEN_CUTS, hidden]
    parts = list(zip(cuts[:-1], cuts[1:]))
    groups = []
    for part, (low, high) in enumerate(parts):
        cols = pl.ds(low, high - low)
        groups.append([
            pltpu.make_async_copy(source.at[:, cols], target.at[:, cols], sems.at[5 * part + k])
            for k, (source, target) in enumerate(zip(far, near))
        ])
        for copy in groups[-1]:
            copy.start()

    for group, (low, high) in zip(groups, parts):
        for copy in group:
            copy.wait()

        @pl.when(core_ref[0] >= 0)
        def _(low=low, high=high):
            cols = slice(low, high)
            for start in range(0, slots, 64):
                at = slice(start, start + 64)
                hid = hid_ref[at, cols].astype(F32)
                gate = gate_ref[at, cols].astype(F32)
                sig = 0.5 * jnp.tanh(0.5 * gate) + 0.5
                silu = gate * sig
                up_term[at, cols] = (hid * silu).astype(BF16)
                gate_term[at, cols] = (
                    hid * up_ref[at, cols].astype(F32) * (sig * (1.0 + gate - silu))
                ).astype(BF16)
            dims = (((1,), (1,)), ((), ()))
            prod = lax.dot_general(
                gate_term[:, cols], gw_ref[:, cols], dims, preferred_element_type=F32
            ) + lax.dot_general(
                up_term[:, cols], uw_ref[:, cols], dims, preferred_element_type=F32
            )
            acc[...] = prod if low == 0 else acc[...] + prod

    width = acc.shape[1]
    count = slots // 16
    main = acc[:, :LANES].reshape(count, 16, LANES)
    side = acc[:, LANES:].reshape(count, 2, 8, width - LANES)
    side = jnp.concatenate([side[:, 0], side[:, 1]], axis=-1)
    packed = jnp.concatenate([main, side], axis=1)
    out_ref[...] = packed.reshape(count * 24, LANES).astype(BF16)


def expert_rows(core, *far):
    slots, hidden = far[0].shape
    width = far[3].shape[0]
    return pl.pallas_call(
        expert_kernel,
        in_specs=[pl.BlockSpec(memory_space=pltpu.SMEM)] + [in_hbm()] * 5,
        out_specs=whole(),
        out_shape=jax.ShapeDtypeStruct((slots * width // LANES, LANES), BF16),
        scratch_shapes=[pltpu.VMEM(array.shape, BF16) for array in far]
        + [pltpu.VMEM((slots, hidden), BF16)] * 2
        + [
            pltpu.VMEM((slots, width), F32),
            pltpu.SemaphoreType.DMA((5 * len(HIDDEN_CUTS),)),
        ],
        compiler_params=params(32 * MIB),
        cost_estimate=pl.CostEstimate(
            flops=4 * slots * hidden * width,
            bytes_accessed=2 * hidden * (3 * slots + 2 * width),
            transcendentals=slots * hidden,
        ),
        name="expert_rows",
    )(core, *map(hold, far))


def chip_sum_kernel(place_ref, own_ref, got_ref, _, keep_ref, *send_refs, full):
    send_refs = send_refs[:3]
    place = place_ref[0]
    for y in range(keep_ref.shape[0] // full):
        at = slice(y * full, (y + 1) * full)
        for turn, ref in enumerate((keep_ref, *send_refs)):
            start = pl.multiple_of((4 * y + (place ^ turn)) * full, 32)
            block = pl.ds(start, full)
            total = own_ref[block, :].astype(F32) + got_ref[block, :].astype(F32)
            ref[at, :] = total.astype(ref.dtype)


def square_sum_kernel(y_ref, keep_ref, *refs, full):
    got, out = refs[:3], refs[3:]
    parts = keep_ref.shape[0] // full
    for step in range(parts):
        start = pl.multiple_of(((y_ref[0] + step) & (parts - 1)) * full, 32)
        block = pl.ds(start, full)
        total = keep_ref[block, :]
        for ref in got:
            total += ref[block, :].astype(F32)
        out[step][...] = total.astype(out[step].dtype)


def write_proj(core_ref, keep_ref, got, out_ref):
    rows = out_ref.shape[0]
    core = core_ref[0]
    total = keep_ref[...]
    for ref in got:
        total += ref[...].astype(F32)
    main, packed = total[:rows], total[rows:]
    half = jnp.concatenate([packed, pltpu.roll(packed, LANES // 2, 1)], axis=0)
    turned = pltpu.roll(main, LANES // 2, 1)
    out_ref[:, :LANES] = jnp.where(core == 0, main, jnp.where(low_lanes(rows), half, turned))
    out_ref[:, LANES:] = jnp.where(core == 0, half, turned)[:, :rows - LANES]


def write_input(picks_ref, residual_ref, got_ref, out_ref):
    experts = got_ref.shape[0] // 48
    got = got_ref[...].astype(F32).reshape(experts, 2, 24, LANES)
    both = got[:, 0] + got[:, 1]
    main = both[:, :16].reshape(experts * 16, LANES)
    side = both[:, 16:].reshape(experts * 8, LANES)

    def dot(start, values):
        return lax.dot_general(
            picks_ref[start:start + values.shape[0], :], values, (((0,), (0,)), ((), ())),
            precision=lax.Precision.HIGHEST, preferred_element_type=F32,
        )

    main_sum = dot(0, main)
    upper = dot(experts * 16, side)
    lower = dot(experts * 24, side)
    side_sum = upper + pltpu.roll(lower, LANES // 2, 1)
    rest = out_ref.shape[1] - LANES
    out_ref[:, :LANES] = (residual_ref[:, :LANES].astype(F32) + main_sum).astype(BF16)
    out_ref[:, LANES:] = (residual_ref[:, LANES:].astype(F32) + side_sum[:, :rest]).astype(BF16)


def last_kernel(core_ref, keep_ref, *refs):
    got, routed, (input_ref, proj_ref) = refs[:-5], refs[-5:-2], refs[-2:]
    write_input(*routed, input_ref)
    write_proj(core_ref, keep_ref, got, proj_ref)


def shards(ids, weights, residual, hid, gate, up, gw, uw, ctx, grad, n_fsdp):
    me = lax.axis_index("fsdp")
    core = (me & 1).reshape(1)
    place = ((me >> 1) & 3).reshape(1)
    y2 = (me >> 3).reshape(1)
    rows = ctx.shape[1]
    full = rows * rows // LANES
    parts = n_fsdp // 8
    smem = pl.BlockSpec(memory_space=pltpu.SMEM)

    def swap(array, bits):
        return lax.ppermute(array, "fsdp", [(j, j ^ bits) for j in range(n_fsdp)])

    def shift(array, step):
        return lax.ppermute(
            array, "fsdp", [(j, (j + 8 * step) % n_fsdp) for j in range(n_fsdp)]
        )

    experts = (hid[0], gate[0], up[0], gw[0], uw[0])
    own, send, picks, residual = front(core, ids.T, weights.T, ctx.T, grad, residual)
    got = swap(send, 1)
    rows_out = expert_rows(core, *experts)

    quarter = jax.ShapeDtypeStruct((parts * full, LANES), BF16)
    keep, *square_send, rows_out = pl.pallas_call(
        functools.partial(chip_sum_kernel, full=full),
        in_specs=[smem, whole(), whole(), pl.BlockSpec(memory_space=pl.ANY)],
        out_specs=[whole()] * 4 + [pl.BlockSpec(memory_space=pl.ANY)],
        out_shape=[jax.ShapeDtypeStruct(quarter.shape, F32)] + [quarter] * 3
        + [jax.ShapeDtypeStruct(rows_out.shape, BF16)],
        input_output_aliases={3: 4},
        compiler_params=params(4 * MIB),
        name="chip_sum",
    )(place, own, got, rows_out)
    square_got = [swap(square_send[k - 1], 2 * k) for k in (1, 3, 2)]
    received = lax.all_to_all(
        rows_out.reshape(-1, 24, LANES), "ep", 0, 0, tiled=True
    ).reshape(rows_out.shape)
    block = jax.ShapeDtypeStruct((full, LANES), BF16)
    keep, *y_send = pl.pallas_call(
        functools.partial(square_sum_kernel, full=full),
        in_specs=[smem] + [whole()] * 4,
        out_specs=[whole()] * parts,
        out_shape=[jax.ShapeDtypeStruct(block.shape, F32)] + [block] * (parts - 1),
        compiler_params=params(4 * MIB),
        cost_estimate=pl.CostEstimate(flops=10**10, bytes_accessed=MIB, transcendentals=0),
        name="square_sum",
    )(y2, keep, *square_got)
    y_got = [shift(y_send[k - 1], k) for k in (1, 3, 2)]

    input_grad, proj_weight_grad = pl.pallas_call(
        last_kernel,
        in_specs=[smem] + [whole()] * (parts + 3),
        out_specs=[whole()] * 2,
        out_shape=[
            jax.ShapeDtypeStruct(residual.shape, BF16),
            jax.ShapeDtypeStruct((rows, rows), F32),
        ],
        compiler_params=params(8 * MIB),
        name="last",
    )(core, keep, *y_got, picks, residual, received)
    return input_grad, proj_weight_grad


def solution(mesh):
    return jax.shard_map(
        functools.partial(shards, n_fsdp=mesh.shape["fsdp"]),
        mesh=mesh,
        in_specs=(
            P("ep", None),
            P("ep", None),
            P("ep", "fsdp"),
            P("ep", None, None),
            P("ep", None, None),
            P("ep", None, None),
            P("ep", "fsdp", None),
            P("ep", "fsdp", None),
            P("fsdp", "ep"),
            P("fsdp", None),
        ),
        out_specs=(P("ep", "fsdp"), P("ep", "fsdp")),
        check_vma=False,
    )
```
